128 devices in a mesh: section: 2 (over z_hi), seq: 8 (over y, z_lo), tensor: 8 (over x, core).
Axes of the slice: x: 4, y: 4, z: 4 (z_hi: 2, z_lo: 2; z = z_hi * 2 + z_lo), core: 2. Of those that a mesh axis runs over, the one named last changes fastest.
Arguments:
- ends: bfloat16 [2, 1024, 9, 1024], P('section', ('seq', 'tensor')), may hold values from -6 to 6
- w_qkv: bfloat16 [2, 1024, 3072], P('section', 'seq', 'tensor'), may hold values from -0.25 to 0.25
- qv_bias: bfloat16 [2, 32, 64], P('section', 'tensor', 'seq'), may hold values from -2.5 to 2.5
- w_proj: bfloat16 [2, 1024, 1024], P('section', 'tensor', 'seq'), may hold values from -0.1875 to 0.1875
- w_fc1: bfloat16 [2, 1024, 4096], P('section', 'seq', 'tensor'), may hold values from -0.1875 to 0.1875
- fc1_bias: bfloat16 [2, 64, 64], P('section', 'tensor', 'seq'), may hold values from -2.5 to 2.5
- w_fc2: bfloat16 [2, 4096, 1024], P('section', 'tensor', 'seq'), may hold values from -0.09375 to 0.09375
- vectors: float32 [2, 8, 1024], P('section', None, ('seq', 'tensor')), may hold values from -1 to 1.6, as said below
Outputs:
- ends_out: bfloat16 [2, 1024, 9, 1024], P('section', ('seq', 'tensor'))
- grad_qkv: float32 [2, 1024, 3072], P('section', 'seq', 'tensor')
- grad_qv_bias: float32 [2, 32, 64], P('section', 'tensor', 'seq')
- grad_proj: float32 [2, 1024, 1024], P('section', 'tensor', 'seq')
- grad_fc1: float32 [2, 1024, 4096], P('section', 'seq', 'tensor')
- grad_fc1_bias: float32 [2, 64, 64], P('section', 'tensor', 'seq')
- grad_fc2: float32 [2, 4096, 1024], P('section', 'tensor', 'seq')
- grad_vectors: float32 [2, 8, 1024], P('section', None, ('seq', 'tensor'))
The draws below stay inside these ranges and needn't reach their ends.
Inputs may be any that keep to these rules, and one draw needn't show every extreme that they name: `vectors`: rows 0, 2, 6 and 7 of each layer lie between 0.4 and 1.6.
All inputs are finite; a program needn't handle non-finite values.
Results may differ from the reference program's by a relative error of at most 0.024.
Values may be sent and summed in bfloat16 or wider, within the bound.
No kernel may reach another device: no remote copies, remote signals or barrier semaphores. Data moves between devices by JAX's collectives and lax.ppermute only.
A program may use at most 192 MiB of HBM per device.

```python
import jax
import jax.numpy as jnp
from jax import lax

D = 1024
HEADS = 16
HEAD = 64
FF = 4096
LENGTH = 1024
IMAGES = 9


def draw_vectors(key, part):
    key = jax.random.fold_in(key, 7)
    key_gain, key_shift = jax.random.split(key)
    row_ids = jnp.arange(8)[None, :, None]
    gain_like = (row_ids == 0) | (row_ids == 2) | (row_ids == 6) | (row_ids == 7)
    gain_rows = jax.random.uniform(key_gain, (2, 8, D), jnp.float32, 0.5, 1.5)
    shift_rows = jnp.clip(0.3 * jax.random.normal(key_shift, (2, 8, D), jnp.float32), -1.0, 1.0)
    return jnp.where(gain_like, gain_rows, shift_rows)


def levels(key, shape, pieces, low, top_value):
    def one(dim, parts):
        steps = jax.random.uniform(jax.random.fold_in(jax.random.fold_in(key, 6), dim), (parts,), jnp.float32, low / len(pieces), top_value / len(pieces))
        return jnp.repeat(jnp.exp(steps), shape[dim] // parts).reshape((-1,) + (1,) * (len(shape) - dim - 1))

    factor_of = one(*pieces[0])
    for cut in pieces[1:]:
        factor_of = factor_of * one(*cut)
    return factor_of


def noise(rng, shape, scale, limit, shards=(), held_as=jnp.bfloat16):
    factor_of = levels(rng, shape, shards, -0.22, 0.18) if shards else 1.0
    entries = jax.random.normal(rng, shape, jnp.float32) * scale * factor_of
    return jnp.minimum(jnp.maximum(entries, -limit), limit).astype(held_as)


def setup_inputs(seed: int = 0) -> dict:
    streams_of = jax.random.split(jax.random.key(seed), 9)
    ends = noise(streams_of[0], (2, LENGTH, IMAGES, D), 1.0, 6.0, ((0, 2), (1, 64)))
    w_qkv = noise(streams_of[1], (2, D, 3 * D), (D // 2) ** -0.5, 0.25, ((0, 2), (1, 8), (2, 8)))
    qv_bias = noise(streams_of[2], (2, 2 * HEADS, HEAD), 0.5, 2.5, ((0, 2), (1, 8), (2, 8)))
    w_proj = noise(streams_of[3], (2, D, D), D ** -0.5, 0.1875, ((0, 2), (1, 8), (2, 8)))
    w_fc1 = noise(streams_of[4], (2, D, FF), D ** -0.5, 0.1875, ((0, 2), (1, 8), (2, 8)))
    fc1_bias = noise(streams_of[5], (2, FF // HEAD, HEAD), 0.5, 2.5, ((0, 2), (1, 8), (2, 8)))
    w_fc2 = noise(streams_of[6], (2, FF, D), FF ** -0.5, 0.09375, ((0, 2), (1, 8), (2, 8)))
    vectors = draw_vectors(jax.random.fold_in(streams_of[8], 71), 0)
    return {"ends": ends, "w_qkv": w_qkv, "qv_bias": qv_bias, "w_proj": w_proj, "w_fc1": w_fc1, "fc1_bias": fc1_bias, "w_fc2": w_fc2, "vectors": vectors}


epsilon = 1e-06
highest = lax.Precision.HIGHEST

@jax.custom_vjp
def low(v):
    return lax.optimization_barrier(v.astype(jnp.bfloat16)).astype(jnp.float32)

@jax.custom_vjp
def low_back(v):
    return v

def low_keep(v):
    return (low(v), None)

def low_pass(kept, grad):
    return (grad,)

def back_keep(v):
    return (v, None)

def back_low(kept, grad):
    return (low(grad),)
low.defvjp(low_keep, low_pass)
low_back.defvjp(back_keep, back_low)

def layer_norm(row_data, gain_row, shift_row):
    row_mean = lax.optimization_barrier(jnp.mean(row_data, axis=-1, keepdims=True))
    centred = row_data - row_mean
    row_var = lax.optimization_barrier(jnp.mean(centred * centred, axis=-1, keepdims=True))
    return centred * lax.rsqrt(row_var + epsilon) * gain_row + shift_row

def encoder_layer(row_data, weights):
    w_mix, b_mix, w_out, w_up, b_up, w_down, params = weights
    length, features = row_data.shape
    head_count = b_mix.shape[0] // 2
    head_size = b_mix.shape[1]
    a_low = low(layer_norm(row_data, params[0], params[1]))
    mixed_cols = jnp.dot(a_low, w_mix, precision=highest).reshape(length, head_count, 3, head_size)
    bias_rows = b_mix.reshape(head_count, 2, head_size)
    queries = low_back(low(mixed_cols[:, :, 0] + bias_rows[:, 0]))
    keys_proj = low_back(low(mixed_cols[:, :, 1]))
    values_proj = low_back(low(mixed_cols[:, :, 2] + bias_rows[:, 1]))
    scores = low_back(jnp.einsum('qhe,khe->hqk', queries, keys_proj, precision=highest) * head_size ** (-0.5))
    probs = low(jax.nn.softmax(scores, axis=-1))
    attended = low_back(low(jnp.einsum('hqk,khe->qhe', probs, values_proj, precision=highest)))
    attended = attended.reshape(length, features)
    middle = row_data + params[6] * (low_back(jnp.dot(attended, w_out, precision=highest)) + params[4])
    a2_low = low(layer_norm(middle, params[2], params[3]))
    hidden = low_back(jnp.dot(a2_low, w_up, precision=highest) + b_up.reshape(-1))
    activated = low(jax.nn.gelu(hidden, approximate=False))
    return middle + params[7] * (low_back(jnp.dot(activated, w_down, precision=highest)) + params[5])

def reference(ends, w_qkv, qv_bias, w_proj, w_fc1, fc1_bias, w_fc2, vectors):
    inputs = jnp.transpose(ends[0].astype(jnp.float32), (1, 0, 2))
    cotangent = jnp.transpose(ends[1].astype(jnp.float32), (1, 0, 2))
    params = (w_qkv.astype(jnp.float32), qv_bias.astype(jnp.float32), w_proj.astype(jnp.float32), w_fc1.astype(jnp.float32), fc1_bias.astype(jnp.float32), w_fc2.astype(jnp.float32), vectors)

    def forward_all(images, weights):

        def per_image(one_image):
            first_out = low_back(low(encoder_layer(one_image, tuple((stored[0] for stored in weights)))))
            return low(encoder_layer(first_out, tuple((stored[1] for stored in weights))))
        return lax.map(jax.checkpoint(per_image), images)
    outputs, pullback = jax.vjp(forward_all, inputs, params)
    grad_in, grad_params = pullback(cotangent)
    ends_out = jnp.transpose(jnp.stack([grad_in, outputs]), (0, 2, 1, 3)).astype(jnp.bfloat16)
    return (ends_out, grad_params[0], grad_params[1], grad_params[2], grad_params[3], grad_params[4], grad_params[5], grad_params[6])
```

```python
import jax
import jax.numpy as jnp
from jax import lax
from jax.experimental import pallas as pl
from jax.experimental.pallas import tpu as pltpu
from jax.sharding import PartitionSpec as P

SS = ("section", "seq")
EPS = 1e-6
F32 = jnp.float32
BF = jnp.bfloat16
D = 1024
HEAD = 64
TOK = 128
GROUPS = [0, 1, 2, 3, 4, None, None, None, 5, 6, 7, 8, None, None, None, None]
SLOT = [GROUPS.index(i) for i in range(9)]


def move_x(v, d):
    return lax.ppermute(v, "tensor", [(i, (i + 2 * d) % 8) for i in range(8)])


def move_core(v):
    return lax.ppermute(v, "tensor", [(i, i ^ 1) for i in range(8)])


def joint(y, z):
    return (z // 2) * 8 + y * 2 + z % 2


def move_yz(v, dy, dz):
    return lax.ppermute(
        v,
        SS,
        [
            (joint(y, z), joint((y + dy) % 4, (z + dz) % 4))
            for y in range(4)
            for z in range(4)
        ],
    )


def move_section(v):
    return lax.ppermute(v, "section", [(0, 1), (1, 0)])


def widen(v):
    return jnp.concatenate([v, move_x(v, 1), move_x(v, -1), move_x(v, 2)], 0)


def narrow(v):
    k = v.shape[0] // 4
    far = move_x(v[3 * k :].astype(BF), 2)
    back = move_x(v[k : 2 * k].astype(BF), -1)
    ahead = move_x(v[2 * k : 3 * k].astype(BF), 1)
    return v[:k].astype(F32) + back.astype(F32) + ahead.astype(F32) + far.astype(F32)


def dot(a, b, dims, out=F32):
    return lax.dot_general(a, b, (dims, ((), ())), preferred_element_type=F32).astype(out)


def attend_kernel(q_ref, k0_ref, v0_ref, k1_ref, v1_ref, o_ref, lse_ref):
    rows = q_ref.shape[0]
    lane = lax.broadcasted_iota(jnp.int32, (rows, 128), 1)
    k = jnp.concatenate([k0_ref[...], k1_ref[...]], 0)
    v = jnp.concatenate([v0_ref[...], v1_ref[...]], 0)
    q = q_ref[...] * jnp.asarray(0.125, BF)
    zero = jnp.zeros_like(q)
    outs = []
    for h in range(2):
        mine = (lane < HEAD) if h == 0 else (lane >= HEAD)
        qh = jnp.where(mine, q, zero)
        s = lax.dot_general(k, qh, (((1,), (1,)), ((), ())), preferred_element_type=F32)
        top = jnp.max(s, axis=0, keepdims=True)
        p = jnp.exp(s - top)
        total = jnp.sum(p, axis=0, keepdims=True)
        o = lax.dot_general(v, p.astype(BF), (((0,), (0,)), ((), ())), preferred_element_type=F32)
        outs.append(o * (1.0 / total))
        lse_ref[0, h : h + 1, :] = top + jnp.log(total)
    sub = lax.broadcasted_iota(jnp.int32, outs[0].shape, 0)
    o_ref[...] = jnp.where(sub < HEAD, outs[0], outs[1]).T.astype(BF)


def attend(q, k0, v0, k1, v1):
    rows = 256
    n = q.shape[0]
    near = pl.BlockSpec((n, 128), lambda p, r: (0, p))
    away = pl.BlockSpec((n, 128), lambda p, r: (0, 1 - p))
    here = pl.BlockSpec((rows, 128), lambda p, r: (r, p))
    return pl.pallas_call(
        attend_kernel,
        grid=(2, n // rows),
        in_specs=[here, near, near, away, away],
        out_specs=[here, pl.BlockSpec((1, 8, rows), lambda p, r: (p, 0, r))],
        out_shape=[
            jax.ShapeDtypeStruct((n, 256), BF),
            jax.ShapeDtypeStruct((2, 8, n), F32),
        ],
        compiler_params=pltpu.CompilerParams(vmem_limit_bytes=40 * 2**20),
        cost_estimate=pl.CostEstimate(
            flops=4 * 4 * n * 2 * n * 256, bytes_accessed=12 * n * 256, transcendentals=8 * n * n
        ),
        name="attend",
    )(q, k0, v0, k1, v1)


def attend_back_kernel(
    q_ref, k0_ref, v0_ref, k1_ref, v1_ref, do_ref, lse_ref,
    dq_ref, dk0_ref, dv0_ref, dk1_ref, dv1_ref, dk_acc, dv_acc,
):
    r = pl.program_id(1)
    rows = q_ref.shape[0]
    n = k0_ref.shape[0]
    lane = lax.broadcasted_iota(jnp.int32, (rows, 128), 1)
    k = jnp.concatenate([k0_ref[...], k1_ref[...]], 0)
    v = jnp.concatenate([v0_ref[...], v1_ref[...]], 0)
    q = q_ref[...] * jnp.asarray(0.125, BF)
    do = do_ref[...]
    zero = jnp.zeros_like(q)
    dqs = []
    dk = jnp.zeros((2 * n, 128), F32)
    dv = jnp.zeros((2 * n, 128), F32)
    for h in range(2):
        mine = (lane < HEAD) if h == 0 else (lane >= HEAD)
        qh = jnp.where(mine, q, zero)
        doh = jnp.where(mine, do, zero)
        s = lax.dot_general(k, qh, (((1,), (1,)), ((), ())), preferred_element_type=F32)
        p = jnp.exp(s - lse_ref[0, h : h + 1, :])
        dv = dv + jnp.dot(p.astype(BF), doh, preferred_element_type=F32)
        dp = lax.dot_general(v, doh, (((1,), (1,)), ((), ())), preferred_element_type=F32)
        delta = jnp.sum(p * dp, axis=0, keepdims=True)
        ds = (p * (dp - delta)).astype(BF)
        dk = dk + jnp.dot(ds, qh, preferred_element_type=F32)
        dqs.append(
            lax.dot_general(k, ds, (((0,), (0,)), ((), ())), preferred_element_type=F32)
        )
    sub = lax.broadcasted_iota(jnp.int32, dqs[0].shape, 0)
    dq_ref[...] = (jnp.where(sub < HEAD, dqs[0], dqs[1]) * 0.125).T.astype(BF)

    @pl.when(r == 0)
    def _():
        dk_acc[...] = dk
        dv_acc[...] = dv

    @pl.when(r > 0)
    def _():
        dk_acc[...] += dk
        dv_acc[...] += dv

    @pl.when(r == pl.num_programs(1) - 1)
    def _():
        dk0_ref[...] = dk_acc[:n]
        dv0_ref[...] = dv_acc[:n]
        dk1_ref[...] = dk_acc[n:].astype(BF)
        dv1_ref[...] = dv_acc[n:].astype(BF)


def attend_back(q, k0, v0, k1, v1, do, lse):
    rows = 256
    n = q.shape[0]
    near = pl.BlockSpec((n, 128), lambda p, r: (0, p))
    away = pl.BlockSpec((n, 128), lambda p, r: (0, 1 - p))
    here = pl.BlockSpec((rows, 128), lambda p, r: (r, p))
    shape = jax.ShapeDtypeStruct
    return pl.pallas_call(
        attend_back_kernel,
        grid=(2, n // rows),
        in_specs=[
            here, near, near, away, away, here,
            pl.BlockSpec((1, 8, rows), lambda p, r: (p, 0, r)),
        ],
        out_specs=[here, near, near, away, away],
        out_shape=[
            shape((n, 256), BF), shape((n, 256), F32), shape((n, 256), F32),
            shape((n, 256), BF), shape((n, 256), BF),
        ],
        scratch_shapes=[pltpu.VMEM((2 * n, 128), F32), pltpu.VMEM((2 * n, 128), F32)],
        compiler_params=pltpu.CompilerParams(vmem_limit_bytes=48 * 2**20),
        cost_estimate=pl.CostEstimate(
            flops=4 * 10 * n * 2 * n * 256, bytes_accessed=26 * n * 256, transcendentals=8 * n * n
        ),
        name="attend_back",
    )(q, k0, v0, k1, v1, do, lse)


def norm_parts(v):
    mean = jnp.mean(v, axis=-1, keepdims=True)
    centred = v - mean
    scale = lax.rsqrt(jnp.mean(centred * centred, axis=-1, keepdims=True) + EPS)
    return centred * scale, scale


def norm(v, gain, shift):
    return norm_parts(v)[0] * gain + shift


def norm_back(v, gain, grad):
    unit, scale = norm_parts(v)
    inner = grad * gain
    part = scale * (
        inner
        - jnp.mean(inner, axis=-1, keepdims=True)
        - unit * jnp.mean(inner * unit, axis=-1, keepdims=True)
    )
    return part, jnp.sum(grad * unit, 0), jnp.sum(grad, 0)


def gelu(v):
    return jax.nn.gelu(v, approximate=False)


def gather_weights(shard, y, z):
    rows, cols = shard.shape
    along_z = jnp.zeros((4, rows, cols), shard.dtype)
    for d in range(4):
        piece = move_yz(shard, 0, d) if d else shard
        along_z = lax.dynamic_update_slice(along_z, piece[None], ((z - d) % 4, 0, 0))
    out = []
    for layer in range(2):
        block = along_z[2 * layer : 2 * layer + 2]
        whole = jnp.zeros((4, 2, rows, cols), shard.dtype)
        for d in range(4):
            piece = move_yz(block, d, 0) if d else block
            whole = lax.dynamic_update_slice(whole, piece[None], ((y - d) % 4, 0, 0, 0))
        whole = whole.reshape(8 * rows, cols)
        out.append((whole, move_core(whole)))
    return out


def forward(x, w, p):
    wq, wo, wu, wd = w
    qkv_bias, up_bias, par = p
    a = norm(x, par[0], par[1]).astype(BF)
    a_wide = widen(a)
    qkv = (dot(a_wide, wq, ((1,), (0,))) + qkv_bias).astype(BF)
    q = jnp.concatenate([qkv[:, 0:128], qkv[:, 384:512]], 1)
    k = jnp.concatenate([qkv[:, 128:256], qkv[:, 512:640]], 1)
    v = jnp.concatenate([qkv[:, 256:384], qkv[:, 640:768]], 1)
    kv = move_core(jnp.concatenate([k, v], 1))
    k1, v1 = kv[:, :256], kv[:, 256:]
    o, lse = attend(q, k, v, k1, v1)
    z = narrow(dot(o, wo, ((1,), (1,)))) + par[4]
    x1 = x + par[6] * z
    a2 = norm(x1, par[2], par[3]).astype(BF)
    a2_wide = widen(a2)
    u = dot(a2_wide, wu, ((1,), (0,))) + up_bias
    gl = gelu(u).astype(BF)
    m = narrow(dot(gl, wd, ((1,), (1,)))) + par[5]
    x2 = x1 + par[7] * m
    return x2, (x, a_wide, q, k, v, k1, v1, o, lse, z, x1, a2_wide, u, gl, m)


def backward(dy, kept, w, p):
    wq, wo, wu, wd = w
    _, _, par = p
    x, a_wide, q, k, v, k1, v1, o, lse, z, x1, a2_wide, u, gl, m = kept
    ds2 = jnp.sum(dy * m, 0)
    dc2 = par[7] * jnp.sum(dy, 0)
    dm = widen((par[7] * dy).astype(BF))
    g_down = dot(dm, gl, ((0,), (0,)))
    dgl = dot(dm, wd, ((1,), (0,)))
    du = jax.vjp(gelu, u)[1](dgl)[0].astype(BF)
    g_up_bias = jnp.sum(du.astype(F32), 0)
    g_up = dot(a2_wide, du, ((0,), (0,)))
    da2 = narrow(dot(du, wu, ((1,), (1,))))
    part, dg2, db2 = norm_back(x1, par[2], da2)
    dx1 = dy + part
    ds1 = jnp.sum(dx1 * z, 0)
    dco = par[6] * jnp.sum(dx1, 0)
    dz = widen((par[6] * dx1).astype(BF))
    g_out = dot(dz, o, ((0,), (0,)))
    do = dot(dz, wo, ((1,), (0,)), BF)
    dq, dk0, dv0, dk1, dv1 = attend_back(q, k, v, k1, v1, do, lse)
    dkv = move_core(jnp.concatenate([dk1, dv1], 1))
    dk = (dk0 + dkv[:, :256].astype(F32)).astype(BF)
    dv = (dv0 + dkv[:, 256:].astype(F32)).astype(BF)
    dqkv = jnp.concatenate(
        [dq[:, :128], dk[:, :128], dv[:, :128], dq[:, 128:], dk[:, 128:], dv[:, 128:]], 1
    )
    g_qkv_bias = jnp.sum(dqkv.astype(F32), 0)
    g_qkv = dot(a_wide, dqkv, ((0,), (0,)))
    da = narrow(dot(dqkv, wq, ((1,), (1,))))
    part, dg1, db1 = norm_back(x, par[0], da)
    dx = dx1 + part
    vec = jnp.stack([dg1, db1, dg2, db2, dco, dc2, ds1, ds2])
    return dx, (g_qkv, g_out, g_up, g_down), (g_qkv_bias, g_up_bias), vec


def scatter_grad(g, seq):
    cols = g.shape[1] // 2
    both = (g[:, :cols] + move_core(g[:, cols:].astype(BF)).astype(F32)).astype(BF)
    rows = both.shape[0] // 8
    total = None
    for d in range(8):
        piece = lax.dynamic_slice(both, (((seq + d) % 8) * rows, 0), (rows, cols))
        if d:
            piece = lax.ppermute(piece, "seq", [(j, (j + d) % 8) for j in range(5)])
        total = piece.astype(F32) if total is None else total + piece.astype(F32)
    return total


def on_device(ends, w_qkv, qv_bias, w_proj, w_fc1, fc1_bias, w_fc2, vectors):
    sec = lax.axis_index("section")
    seq = lax.axis_index("seq")
    ten = lax.axis_index("tensor")
    first = sec == 0
    core = ten % 2
    y = seq // 2
    z = sec * 2 + seq % 2

    by_image = jnp.transpose(ends[0], (1, 0, 2))
    blank = jnp.zeros(by_image.shape[1:], BF)
    send = jnp.stack([blank if g is None else by_image[g] for g in GROUPS])
    got = lax.all_to_all(send, SS, 0, 0, tiled=True)
    x = got[:8].reshape(TOK, D).astype(F32)
    cot = got[8:].reshape(TOK, D).astype(F32)

    flat = jnp.concatenate(
        [
            vectors[0].reshape(-1),
            qv_bias[0].astype(F32).reshape(-1),
            fc1_bias[0].astype(F32).reshape(-1),
            jnp.zeros((32,), F32),
        ]
    ).reshape(2, 128)
    flat = lax.all_to_all(jnp.broadcast_to(flat[None], (8, 2, 128)), "tensor", 0, 0, tiled=True)
    flat = flat.reshape(1, 16, 128)
    flat = lax.all_to_all(jnp.broadcast_to(flat, (16, 16, 128)), SS, 0, 0, tiled=True)
    flat = flat.reshape(2, 8, 8, 256)
    pars = []
    for layer in range(2):
        f = flat[layer]
        par = f[:, :, :128].reshape(8, 8, 8, 16)
        par = jnp.transpose(par, (2, 0, 1, 3)).reshape(8, D)
        sides_q, sides_u = [], []
        for owner in (ten, ten ^ 1):
            b = lax.dynamic_slice(f, (0, owner, 0), (8, 1, 256))[:, 0]
            bq = b[:, 128:160].reshape(8, 2, 2, 8)
            bq = jnp.transpose(bq, (2, 1, 0, 3)).reshape(2, 128)
            sides_q += [bq[0], jnp.zeros((128,), F32), bq[1]]
            bu = b[:, 160:224].reshape(8, 8, 8)
            sides_u.append(jnp.transpose(bu, (1, 0, 2)).reshape(512))
        pars.append((jnp.concatenate(sides_q), jnp.concatenate(sides_u), par))

    own_qkv = jnp.transpose(w_qkv[0].reshape(128, 2, 3, HEAD), (0, 2, 1, 3)).reshape(128, 384)
    near = jnp.concatenate([own_qkv, w_proj[0].T], 1)
    far = jnp.concatenate([w_fc1[0], w_fc2[0].T], 1)
    near = gather_weights(near, y, z)
    far = gather_weights(far, y, z)
    weights = []
    for layer in range(2):
        a, b = near[layer]
        c, d = far[layer]
        weights.append(
            (
                jnp.concatenate([a[:, :384], b[:, :384]], 1),
                jnp.concatenate([a[:, 384:], b[:, 384:]], 1),
                jnp.concatenate([c[:, :512], d[:, :512]], 1),
                jnp.concatenate([c[:, 512:], d[:, 512:]], 1),
            )
        )

    x2, kept0 = forward(x, weights[0], pars[0])
    y0 = x2.astype(BF).astype(F32)
    x2, kept1 = forward(y0, weights[1], pars[1])
    y1 = x2.astype(BF)
    dx, g1, b1, v1 = backward(cot, kept1, weights[1], pars[1])
    dx, g0, b0, v0 = backward(dx.astype(BF).astype(F32), kept0, weights[0], pars[0])
    dx = dx.astype(BF)

    back = jnp.concatenate([dx.reshape(8, 16, D), y1.reshape(8, 16, D)], 0)
    back = lax.all_to_all(back, SS, 0, 0, tiled=True)
    ends_out = jnp.transpose(jnp.stack([back[s] for s in SLOT]), (1, 0, 2))

    grads = []
    for a, b in zip(g0, g1):
        r0, r1 = scatter_grad(a, seq), scatter_grad(b, seq)
        other = move_section(jnp.where(first, r1, r0).astype(BF)).astype(F32)
        grads.append(jnp.where(first, r0, r1) + other)
    g_qkv, g_out, g_up, g_down = grads
    g_qkv = jnp.transpose(g_qkv.reshape(128, 3, 2, HEAD), (0, 2, 1, 3)).reshape(128, 384)

    vec = jnp.stack([v0, v1]).reshape(2, 8, 8, 8, 16)
    vec = jnp.transpose(vec, (3, 0, 2, 1, 4)).reshape(8, 2, 8, 128)
    sides = []
    for side in range(2):
        rows = []
        for gq, gu in (b0, b1):
            gq = gq[384 * side : 384 * side + 384]
            gq = jnp.stack([gq[:128], gq[256:]]).reshape(2, 2, 8, 8)
            gq = jnp.transpose(gq, (2, 1, 0, 3)).reshape(8, 32)
            gu = gu[512 * side : 512 * side + 512].reshape(8, 8, 8)
            gu = jnp.transpose(gu, (1, 0, 2)).reshape(8, 64)
            rows.append(jnp.concatenate([gq, gu, jnp.zeros((8, 32), F32)], 1))
        sides.append(jnp.stack(rows))
    who = jnp.arange(8)[:, None, None, None]
    bias = jnp.where(who == ten, sides[0][None], jnp.where(who == (ten ^ 1), sides[1][None], 0.0))
    small = jnp.concatenate([vec, bias], -1).reshape(8, 32, 128)
    small = lax.all_to_all(small, "tensor", 0, 0, tiled=True)
    small = jnp.sum(small, 0).reshape(16, 2, 128)
    small = lax.all_to_all(small, SS, 0, 0, tiled=True)
    small = jnp.sum(small, 0)
    g_vec = small[0].reshape(8, 16)
    g_qvb = small[1, :32].reshape(4, 8)
    g_upb = small[1, 32:96].reshape(8, 8)
    return (
        ends_out[None],
        g_qkv[None],
        g_qvb[None],
        g_out.T[None],
        g_up[None],
        g_upb[None],
        g_down.T[None],
        g_vec[None],
    )


def solution(mesh):
    placed = (
        P("section", ("seq", "tensor"), None, None),
        P("section", "seq", "tensor"),
        P("section", "tensor", "seq"),
        P("section", "tensor", "seq"),
        P("section", "seq", "tensor"),
        P("section", "tensor", "seq"),
        P("section", "tensor", "seq"),
        P("section", None, ("seq", "tensor")),
    )
    return jax.shard_map(
        on_device, mesh=mesh, in_specs=placed, out_specs=placed, check_vma=False
    )
```

```python
import jax
import jax.numpy as jnp
from jax import lax
from jax.experimental import pallas as pl
from jax.experimental.pallas import tpu as pltpu
from jax.sharding import PartitionSpec as P

SS = ("section", "seq")
EPS = 1e-6
F32 = jnp.float32
BF = jnp.bfloat16
D = 1024
HEAD = 64
TOK = 128
GROUPS = [0, 1, 2, 3, 4, None, None, None, 5, 6, 7, 8, None, None, None, None]
SLOT = [GROUPS.index(i) for i in range(9)]


def move_x(v, d):
    return lax.ppermute(v, "tensor", [(i, (i + 2 * d) % 8) for i in range(8)])


def move_core(v):
    return lax.ppermute(v, "tensor", [(i, i ^ 1) for i in range(8)])


def move_section(v):
    return lax.ppermute(v, "section", [(0, 1), (1, 0)])


def widen(v):
    return v, move_x(v, 1), move_x(v, -1), move_x(v, 2)


def narrow(parts):
    own, back, ahead, far = parts
    return own, move_x(back, -1), move_x(ahead, 1), move_x(far, 2)


def dot(a, b, dims, out=F32):
    return lax.dot_general(a, b, (dims, ((), ())), preferred_element_type=F32).astype(out)


NN = ((1,), (0,))
NT = ((1,), (1,))
TN = ((0,), (0,))


def entire(a):
    zeros = (0,) * len(a.shape)
    return pl.BlockSpec(a.shape, lambda i: zeros, pipeline_mode=pl.Buffered(1))


def part(width, k):
    return pl.BlockSpec((1024, width), lambda i: (0, k), pipeline_mode=pl.Buffered(1))


def whole(kernel, out_shape, *args, name, cols=None):
    return pl.pallas_call(
        kernel,
        grid=(1,),
        out_shape=out_shape,
        in_specs=[entire(a) for a in args] if cols is None else [
            entire(a) if a.shape[1:] != (512,) or a.shape[0] != 1024 else part(*cols) for a in args
        ],
        out_specs=jax.tree.map(entire, out_shape),
        compiler_params=pltpu.CompilerParams(vmem_limit_bytes=60 * 2**20),
        cost_estimate=pl.CostEstimate(flops=0, bytes_accessed=4096, transcendentals=0),
        name=name,
    )(*args)


def out(shape, dtype):
    return jax.ShapeDtypeStruct(shape, dtype)


def row(p_ref, r):
    return jnp.concatenate([p_ref[q, r : r + 1, :] for q in range(8)], axis=1)


def bias_rows(p_ref, side):
    return sum(p_ref[q, 8 + 8 * side : 16 + 8 * side, :] for q in range(8))


def unit_of(v):
    centred = v - jnp.mean(v, axis=-1, keepdims=True)
    scale = lax.rsqrt(jnp.mean(centred * centred, axis=-1, keepdims=True) + EPS)
    return centred * scale, scale


def norm_back(v, gain, grad):
    unit, scale = unit_of(v)
    inner = grad * gain
    part = scale * (
        inner
        - jnp.mean(inner, axis=-1, keepdims=True)
        - unit * jnp.mean(inner * unit, axis=-1, keepdims=True)
    )
    return part, jnp.sum(grad * unit, 0, keepdims=True), jnp.sum(grad, 0, keepdims=True)


def total(own, back, ahead, far):
    return own[...] + back[...].astype(F32) + ahead[...].astype(F32) + far[...].astype(F32)


def start_kernel(x_ref, p_ref, a_ref):
    unit, _ = unit_of(x_ref[...].astype(F32))
    a_ref[...] = (unit * row(p_ref, 0) + row(p_ref, 1)).astype(BF)


def qkv_kernel(a0, a1, a2, a3, w0, w1, p_ref, o_ref, a_ref):
    join_rows((a0, a1, a2, a3), a_ref)
    mix_rows((a0, a1, a2, a3), w0, w1, p_ref, o_ref)


def mix_rows(pieces, w0, w1, p_ref, o_ref):
    for side, w in enumerate((w0, w1)):
        b = bias_rows(p_ref, side)
        b = jnp.concatenate([b[0:1], b[1:2], b[2:3]], axis=1)
        for i, a in enumerate(pieces):
            o_ref[128 * i : 128 * i + 128, 384 * side : 384 * side + 384] = (
                jnp.dot(a[...], w[...], preferred_element_type=F32) + b
            ).astype(BF)


def join_rows(pieces, ref):
    for i, piece in enumerate(pieces):
        ref[128 * i : 128 * i + 128, :] = piece[...]


def first_qkv_kernel(x0, x1, x2, x3, w0, w1, p_ref, o_ref, a_ref):
    pieces = [a_ref.at[128 * i : 128 * i + 128] for i in range(4)]
    for x, a in zip((x0, x1, x2, x3), pieces):
        start_kernel(x, p_ref, a)
    mix_rows(pieces, w0, w1, p_ref, o_ref)


def spread(left, own_ref, others):
    own_ref[...] = left(0)
    for i, ref in enumerate(others):
        ref[...] = left(i + 1).astype(BF)


def spread_out():
    return [out((TOK, D), F32)] + [out((TOK, D), BF)] * 3


def pair_kernel(l0, l1, w0, w1, own, back, ahead, far):
    def left(i):
        at = slice(128 * i, 128 * i + 128)
        return dot(l0[at, :], w0[...], NT) + dot(l1[at, :], w1[...], NT)

    spread(left, own, (back, ahead, far))


def proj_kernel(o, w0, w1, own, back, ahead, far):
    w = jnp.concatenate([w0[...], w1[...]], axis=1)
    spread(lambda i: dot(o[128 * i : 128 * i + 128, :], w, NT), own, (back, ahead, far))


def mixed_kernel(g, w0, w1, own, back, ahead, far):
    w = jnp.concatenate([w0[...], w1[...]], axis=1)
    spread(lambda i: dot(g[128 * i : 128 * i + 128, :], w, NT), own, (back, ahead, far))


def middle_kernel(own, back, ahead, far, x_ref, p_ref, z_ref, x1_ref, a2_ref):
    z = total(own, back, ahead, far) + row(p_ref, 4)
    x1 = x_ref[...].astype(F32) + row(p_ref, 6) * z
    unit, _ = unit_of(x1)
    z_ref[...] = z
    x1_ref[...] = x1
    a2_ref[...] = (unit * row(p_ref, 2) + row(p_ref, 3)).astype(BF)


def up_kernel(a0, a1, a2, a3, w0, w1, p_ref, act0, act1, slope0, slope1, a_ref):
    join_rows((a0, a1, a2, a3), a_ref)
    for side, (w, act, slope) in enumerate(((w0, act0, slope0), (w1, act1, slope1))):
        b = bias_rows(p_ref, side)
        b = jnp.concatenate([b[3:4], b[4:5], b[5:6], b[6:7]], axis=1)
        for i, a in enumerate((a0, a1, a2, a3)):
            at = slice(128 * i, 128 * i + 128)
            u = jnp.dot(a[...], w[...], preferred_element_type=F32) + b
            half = 0.5 * (1.0 + lax.erf(u * (0.5**0.5)))
            act[at, :] = (u * half).astype(BF)
            slope[at, :] = (half + u * jnp.exp(-0.5 * u * u) * 0.3989422804014327).astype(BF)


def mlp_kernel(
    a0, a1, a2, a3, u0, u1, d0, d1, p_ref, act0, act1, slope0, slope1, a_ref, own, back, ahead, far
):
    up_kernel(a0, a1, a2, a3, u0, u1, p_ref, act0, act1, slope0, slope1, a_ref)
    pair_kernel(act0, act1, d0, d1, own, back, ahead, far)


def mlp_back_kernel(
    d0, d1, d2, d3, w0, w1, u0, u1, s0, s1, du0, du1, sums, d_ref, own, back, ahead, far
):
    join_rows((d0, d1, d2, d3), d_ref)
    du_kernel(d0, d1, d2, d3, w0, w1, s0, s1, du0, du1, sums)
    pair_kernel(du0, du1, u0, u1, own, back, ahead, far)


def end_kernel(own, back, ahead, far, x1_ref, p_ref, m_ref, y_ref):
    m = total(own, back, ahead, far) + row(p_ref, 5)
    m_ref[...] = m
    y_ref[...] = (x1_ref[...] + row(p_ref, 7) * m).astype(BF)


def end_next_kernel(own, back, ahead, far, x1_ref, p_ref, next_ref, m_ref, y_ref, a_ref):
    end_kernel(own, back, ahead, far, x1_ref, p_ref, m_ref, y_ref)
    start_kernel(y_ref, next_ref, a_ref)


def turn_kernel(*refs):
    scale = row(refs[4], 7)
    for dy, dm in zip(refs[:4], refs[5:]):
        dm[...] = (scale * dy[...].astype(F32)).astype(BF)


def du_kernel(d0, d1, d2, d3, w0, w1, s0, s1, du0, du1, sums_ref):
    for side, (w, slope, du_ref) in enumerate(((w0, s0, du0), (w1, s1, du1))):
        acc = jnp.zeros((1, 512), F32)
        for i, d in enumerate((d0, d1, d2, d3)):
            at = slice(128 * i, 128 * i + 128)
            du = (jnp.dot(d[...], w[...], preferred_element_type=F32) * slope[at, :].astype(F32)).astype(BF)
            du_ref[at, :] = du
            acc = acc + jnp.sum(du.astype(F32), 0, keepdims=True)
        for k in range(4):
            sums_ref[side, k : k + 1, :] = acc[:, 128 * k : 128 * k + 128]
        sums_ref[side, 4:, :] = jnp.zeros((4, 128), F32)


def middle_back_kernel(own, back, ahead, far, x1_ref, dy_ref, z_ref, p_ref, dx1_ref, dz_ref, rows_ref):
    part, dg, db = norm_back(x1_ref[...], row(p_ref, 2), total(own, back, ahead, far))
    dx1 = dy_ref[...].astype(F32) + part
    scale = row(p_ref, 6)
    dx1_ref[...] = dx1
    dz_ref[...] = (scale * dx1).astype(BF)
    rows_ref[0:1, :] = dg
    rows_ref[1:2, :] = db
    rows_ref[2:3, :] = scale * jnp.sum(dx1, 0, keepdims=True)
    rows_ref[3:4, :] = jnp.sum(dx1 * z_ref[...], 0, keepdims=True)


def do_kernel(d0, d1, d2, d3, w0, w1, o_ref, d_ref):
    join_rows((d0, d1, d2, d3), d_ref)
    w = jnp.concatenate([w0[...], w1[...]], axis=1)
    for i, d in enumerate((d0, d1, d2, d3)):
        o_ref[128 * i : 128 * i + 128, :] = jnp.dot(d[...], w, preferred_element_type=F32).astype(BF)


def pack_out(out_ref, ends, vec, bias_ref):
    for q in range(8):
        for k in range(8):
            out_ref[q, 16 * k : 16 * k + 16, :] = ends[16 * q : 16 * q + 16, 128 * k : 128 * k + 128]
        part = [v[:, 128 * q : 128 * q + 128] for v in vec]
        part = jnp.concatenate(part + [bias_ref[0], bias_ref[1]], axis=0)
        high = part.astype(BF).astype(F32)
        out_ref[q, 128:176, :] = jnp.concatenate([high, part - high], axis=0).astype(BF)


def first_back(da, x_ref, dx1_ref, p_ref, dy_ref, m_ref, mid_ref):
    part, dg, db = norm_back(x_ref[...].astype(F32), row(p_ref, 0), total(*da))
    dy = dy_ref[...].astype(F32)
    vec = [
        dg, db, mid_ref[0:1, :], mid_ref[1:2, :], mid_ref[2:3, :],
        row(p_ref, 7) * jnp.sum(dy, 0, keepdims=True),
        mid_ref[3:4, :],
        jnp.sum(dy * m_ref[...], 0, keepdims=True),
    ]
    return (dx1_ref[...] + part).astype(BF), vec


def last_back_kernel(own, back, ahead, far, x, dx1, p, dy, m, mid, bias, out_ref):
    dx, vec = first_back((own, back, ahead, far), x, dx1, p, dy, m, mid)
    pack_out(out_ref, dx, vec, bias)


def next_back_kernel(
    own, back, ahead, far, x, dx1, p, dy, m, mid, bias, y_ref, next_ref, out_ref, dx_ref, dm_ref
):
    dx, vec = first_back((own, back, ahead, far), x, dx1, p, dy, m, mid)
    dx_ref[...] = dx
    dm_ref[...] = (row(next_ref, 7) * dx.astype(F32)).astype(BF)
    pack_out(out_ref, y_ref[...], vec, bias)


def attend_kernel(q_ref, k0_ref, v0_ref, k1_ref, v1_ref, o_ref, lse_ref):
    rows = q_ref.shape[0]
    lane = lax.broadcasted_iota(jnp.int32, (rows, 128), 1)
    k = jnp.concatenate([k0_ref[...], k1_ref[...]], 0)
    v = jnp.concatenate([v0_ref[...], v1_ref[...]], 0)
    q = q_ref[...] * jnp.asarray(0.125, BF)
    zero = jnp.zeros_like(q)
    outs = []
    for h in range(2):
        mine = (lane < HEAD) if h == 0 else (lane >= HEAD)
        qh = jnp.where(mine, q, zero)
        s = lax.dot_general(k, qh, (((1,), (1,)), ((), ())), preferred_element_type=F32)
        top = jnp.max(s, axis=0, keepdims=True)
        p = jnp.exp(s - top)
        total = jnp.sum(p, axis=0, keepdims=True)
        o = lax.dot_general(v, p.astype(BF), (((0,), (0,)), ((), ())), preferred_element_type=F32)
        outs.append(o * (1.0 / total))
        lse_ref[0, h : h + 1, :] = top + jnp.log(total)
    sub = lax.broadcasted_iota(jnp.int32, outs[0].shape, 0)
    o_ref[...] = jnp.where(sub < HEAD, outs[0], outs[1]).T.astype(BF)


def column(rows, part, swap=False, tall=False):
    if swap:
        return pl.BlockSpec((rows, 128), lambda p, r: (0, 3 * (1 - p) + part))
    if tall:
        return pl.BlockSpec((rows, 128), lambda p, r: (0, 3 * p + part))
    return pl.BlockSpec((rows, 128), lambda p, r: (r, 3 * p + part))


def attend(qkv, away):
    rows = 256
    n = qkv.shape[0]
    return pl.pallas_call(
        attend_kernel,
        grid=(2, n // rows),
        in_specs=[
            column(rows, 0),
            column(n, 1, tall=True), column(n, 2, tall=True),
            column(n, 1, swap=True), column(n, 2, swap=True),
        ],
        out_specs=[
            pl.BlockSpec((rows, 128), lambda p, r: (r, p)),
            pl.BlockSpec((1, 8, rows), lambda p, r: (p, 0, r)),
        ],
        out_shape=[
            jax.ShapeDtypeStruct((n, 256), BF),
            jax.ShapeDtypeStruct((2, 8, n), F32),
        ],
        compiler_params=pltpu.CompilerParams(vmem_limit_bytes=60 * 2**20),
        cost_estimate=pl.CostEstimate(flops=0, bytes_accessed=4096, transcendentals=0),
        name="attend",
    )(qkv, qkv, qkv, away, away)


def attend_back_kernel(
    q_ref, k0_ref, v0_ref, k1_ref, v1_ref, do_ref, lse_ref,
    dq_ref, near_ref, far_ref, dk_acc, dv_acc,
):
    r = pl.program_id(1)
    rows = q_ref.shape[0]
    n = k0_ref.shape[0]
    lane = lax.broadcasted_iota(jnp.int32, (rows, 128), 1)
    k = jnp.concatenate([k0_ref[...], k1_ref[...]], 0)
    v = jnp.concatenate([v0_ref[...], v1_ref[...]], 0)
    q = q_ref[...] * jnp.asarray(0.125, BF)
    do = do_ref[...]
    zero = jnp.zeros_like(q)
    dqs = []
    dk = jnp.zeros((2 * n, 128), F32)
    dv = jnp.zeros((2 * n, 128), F32)
    for h in range(2):
        mine = (lane < HEAD) if h == 0 else (lane >= HEAD)
        qh = jnp.where(mine, q, zero)
        doh = jnp.where(mine, do, zero)
        s = lax.dot_general(k, qh, (((1,), (1,)), ((), ())), preferred_element_type=F32)
        p = jnp.exp(s - lse_ref[0, h : h + 1, :])
        dv = dv + jnp.dot(p.astype(BF), doh, preferred_element_type=F32)
        dp = lax.dot_general(v, doh, (((1,), (1,)), ((), ())), preferred_element_type=F32)
        delta = jnp.sum(p * dp, axis=0, keepdims=True)
        ds = (p * (dp - delta)).astype(BF)
        dk = dk + jnp.dot(ds, qh, preferred_element_type=F32)
        dqs.append(
            lax.dot_general(k, ds, (((0,), (0,)), ((), ())), preferred_element_type=F32)
        )
    sub = lax.broadcasted_iota(jnp.int32, dqs[0].shape, 0)
    dq_ref[...] = (jnp.where(sub < HEAD, dqs[0], dqs[1]) * 0.125).T.astype(BF)

    @pl.when(r == 0)
    def _():
        dk_acc[...] = dk
        dv_acc[...] = dv

    @pl.when(r > 0)
    def _():
        dk_acc[...] += dk
        dv_acc[...] += dv

    @pl.when(r == pl.num_programs(1) - 1)
    def _():
        near_ref[:, :128] = dk_acc[:n]
        near_ref[:, 128:] = dv_acc[:n]
        far_ref[:, :128] = dk_acc[n:].astype(BF)
        far_ref[:, 128:] = dv_acc[n:].astype(BF)


def attend_back(qkv, away, do, lse):
    rows = 256
    n = qkv.shape[0]
    here = pl.BlockSpec((rows, 128), lambda p, r: (r, p))
    shape = jax.ShapeDtypeStruct
    return pl.pallas_call(
        attend_back_kernel,
        grid=(2, n // rows),
        in_specs=[
            column(rows, 0),
            column(n, 1, tall=True), column(n, 2, tall=True),
            column(n, 1, swap=True), column(n, 2, swap=True),
            here,
            pl.BlockSpec((1, 8, rows), lambda p, r: (p, 0, r)),
        ],
        out_specs=[
            here,
            pl.BlockSpec((n, 256), lambda p, r: (0, p)),
            pl.BlockSpec((n, 256), lambda p, r: (0, 1 - p)),
        ],
        out_shape=[shape((n, 256), BF), shape((n, 512), F32), shape((n, 512), BF)],
        scratch_shapes=[pltpu.VMEM((2 * n, 128), F32), pltpu.VMEM((2 * n, 128), F32)],
        compiler_params=pltpu.CompilerParams(vmem_limit_bytes=60 * 2**20),
        cost_estimate=pl.CostEstimate(flops=0, bytes_accessed=4096, transcendentals=0),
        name="attend_back",
    )(qkv, qkv, qkv, away, away, do, lse)


def join_da_kernel(dq, near, far_in, up, w0, w1, dqkv, sums, own, back, ahead, far):
    join_kernel(dq, near, far_in, up, dqkv, sums)
    mixed_kernel(dqkv, w0, w1, own, back, ahead, far)


def join_kernel(dq_ref, near_ref, far_ref, up_ref, out_ref, sums_ref):
    for p in range(2):
        dkv = (near_ref[:, 256 * p : 256 * p + 256] + far_ref[:, 256 * p : 256 * p + 256].astype(F32)).astype(BF)
        dq = dq_ref[:, 128 * p : 128 * p + 128]
        out_ref[:, 384 * p : 384 * p + 128] = dq
        out_ref[:, 384 * p + 128 : 384 * p + 384] = dkv
        sums_ref[p, 0:1, :] = jnp.sum(dq.astype(F32), 0, keepdims=True)
        kv = jnp.sum(dkv.astype(F32), 0, keepdims=True)
        sums_ref[p, 1:2, :] = kv[:, :128]
        sums_ref[p, 2:3, :] = kv[:, 128:]
        sums_ref[p, 3:7, :] = up_ref[p, 0:4, :]
        sums_ref[p, 7:8, :] = jnp.zeros((1, 128), F32)


MM = 2 * 512 * 1024 * 1024


def after(value, *events):
    return lax.optimization_barrier((value, *events))[0]


def gather(shard, *events):
    full = after(jnp.broadcast_to(shard[None], (8, 128, 512)), *events)
    return lax.all_to_all(full, "seq", 0, 0, tiled=True).reshape(1024, 512)


def gather_slow(shard, *events):
    return lax.all_gather(after(shard, *events), "seq", axis=0, tiled=True)


def scatter_slow(g):
    return lax.psum_scatter(g, "seq", scatter_dimension=0, tiled=True)


def sides(full):
    return full, move_core(full)


def scatter(g, *events):
    return lax.all_to_all(after(g, *events), "seq", 0, 0, tiled=True).reshape(8, 128, -1)


def add_up(blocks):
    return jnp.sum(blocks.astype(F32), 0)


def core_sum(own, other):
    return (own + move_core(other).astype(F32)).astype(BF)


def hold(parts, *events):
    return (*parts[:-1], after(parts[-1], *events))


def mix(a_wide, near, p):
    return whole(qkv_kernel, [out((512, 768), BF), all_rows()], *a_wide, *near, p, name="qkv", cols=(384, 0))


def mix_first(x_wide, near, p):
    shapes = [out((512, 768), BF), all_rows()]
    return whole(first_qkv_kernel, shapes, *x_wide, *near, p, name="first_qkv", cols=(384, 0))


def proj(o, near):
    return whole(proj_kernel, spread_out(), o, *near, name="proj", cols=(128, 3))


def middle(z, x, p):
    return whole(
        middle_kernel, [out((TOK, D), F32)] * 2 + [out((TOK, D), BF)], *z, x, p, name="middle"
    )


def all_rows():
    return out((512, D), BF)


def act_out():
    return [out((512, 512), BF)] * 4 + [all_rows()]


def mlp_back(dm_wide, act, w):
    _, up, down = w
    *du, sums, dm_all, own, back, ahead, far = whole(
        mlp_back_kernel,
        [out((512, 512), BF)] * 2 + [out((2, 8, 128), F32), all_rows()] + spread_out(),
        *dm_wide, *down, *up, *act[2:4], name="mlp_back",
    )
    return du, sums, dm_all, (own, back, ahead, far)


def middle_back(da2, x1, dy, z, p):
    return whole(
        middle_back_kernel, [out((TOK, D), F32), out((TOK, D), BF), out((4, D), F32)],
        *da2, x1, dy, z, p, name="middle_back",
    )


def pair_grad(rows, left, right):
    return core_sum(dot(rows, left, TN), dot(rows, right, TN, BF))


def near_grad(a_all, dqkv, dz_all, o):
    own = jnp.concatenate([dot(a_all, dqkv[:, :384], TN), dot(dz_all, o[:, :128], TN)], 1)
    other = jnp.concatenate(
        [dot(a_all, dqkv[:, 384:], TN, BF), dot(dz_all, o[:, 128:], TN, BF)], 1
    )
    return core_sum(own, other)


def back_to(dz_wide, near):
    return whole(do_kernel, [out((512, 256), BF), all_rows()], *dz_wide, *near, name="do", cols=(128, 3))


def join_da(dq, nearby, far, up_sums, near):
    dqkv, sums, *da = whole(
        join_da_kernel,
        [out((512, 768), BF), out((2, 8, 128), F32)] + spread_out(),
        dq, nearby, far, up_sums, *near, name="join_da", cols=(384, 0),
    )
    return dqkv, sums, da


def on_device(ends, w_qkv, qv_bias, w_proj, w_fc1, fc1_bias, w_fc2, vectors):
    sec = lax.axis_index("section")
    seq = lax.axis_index("seq")
    ten = lax.axis_index("tensor")
    first = sec == 0

    lane = jnp.arange(128)[None, :]
    vec = jnp.where(lane // 16 == ten, jnp.tile(vectors[0], (1, 8)), 0.0)
    here = (jnp.arange(8) == seq).astype(F32)[None, :, None]
    qv = qv_bias[0].astype(F32).reshape(2, 2, 8)
    qv = jnp.stack([qv[:, 0], jnp.zeros((2, 8), F32), qv[:, 1]])
    qv = (qv.reshape(6, 1, 8) * here).reshape(3, 128)
    fb = (fc1_bias[0].astype(F32)[:, None, :] * here).reshape(4, 128)
    bias = jnp.concatenate([qv, fb, jnp.zeros((1, 128), F32)], 0)
    both = move_core(jnp.concatenate([vec, bias], 0))
    small = jnp.concatenate([vec + both[:8], bias, both[8:]], 0)
    high = lax.reduce_precision(small, 8, 7)
    mid = lax.reduce_precision(small - high, 8, 7)
    parts = jnp.concatenate([high, mid, small - high - mid, jnp.zeros((8, 128), F32)], 0).astype(BF)

    by_image = jnp.transpose(ends[0].reshape(16, 9, 8, 128), (1, 2, 0, 3)).reshape(9, 128, 128)
    blank = jnp.zeros((128, 128), BF)
    send = jnp.stack([blank if g is None else by_image[g] for g in GROUPS])
    send = jnp.concatenate([send, jnp.broadcast_to(parts[None], (16, 80, 128))], 1)
    got = lax.all_to_all(send, SS, 0, 0, tiled=True)
    x, cot = (
        jnp.transpose(v.reshape(8, 8, 16, 128), (0, 2, 1, 3)).reshape(TOK, D)
        for v in (got[:8, :128], got[8:, :128])
    )
    small = got[:, 128:].astype(F32)
    small = small[:, :24] + small[:, 24:48] + small[:, 48:72]
    vec = small[:, :8]
    vec = vec + move_x(vec, 1) + move_x(vec, -1) + move_x(vec, 2)
    pars = jnp.concatenate([vec, small[:, 8:]], 1)
    p0, p1 = pars[:8], pars[8:]

    own_qkv = jnp.transpose(w_qkv[0].reshape(128, 2, 3, HEAD), (0, 2, 1, 3)).reshape(128, 384)
    shard = jnp.concatenate([own_qkv, w_proj[0].T, w_fc1[0], w_fc2[0].T], 1)
    moved = move_section(shard)
    shards = jnp.where(first, shard, moved), jnp.where(first, moved, shard)
    shards = [[v[:, 512 * k : 512 * k + 512] for v in shards] for k in range(3)]

    def to_owner(a, b):
        other = move_section(jnp.where(first, b, a).astype(BF)).astype(F32)
        return jnp.where(first, a, b) + other

    near0 = gather(shards[0][0], got)
    x_wide0 = widen(x)
    cot_wide = widen(after(cot, *x_wide0))
    near0 = sides(after(near0, p0, *x_wide0))
    qkv0, a_all0 = mix_first(x_wide0, near0, p0)
    away0 = move_core(qkv0)
    up0 = gather(shards[1][0], near0[0], p0)
    o0, lse0 = attend(qkv0, away0)
    dm_wide1 = whole(turn_kernel, [out((TOK, D), BF)] * 4, *cot_wide, p1, name="turn")
    z = proj(o0, near0)
    down0 = gather(shards[2][0], up0, z[3])
    near1 = gather_slow(shards[0][1], z[3])
    up0 = sides(after(up0, z[3], *cot_wide))
    z0, x10, a2 = middle(narrow(z), x, p0)
    down0 = sides(after(down0, x10))
    a2_wide0 = widen(a2)
    *act0, o_, b_, a_, f_ = whole(
        mlp_kernel, act_out() + spread_out(), *a2_wide0, *up0, *down0, p0,
        name="mlp",
    )
    near1 = sides(after(near1, f_))
    up1 = gather_slow(shards[1][1], f_)
    m0, y0, a = whole(
        end_next_kernel, [out((TOK, D), F32), out((TOK, D), BF), out((TOK, D), BF)],
        *narrow((o_, b_, a_, f_)), x10, p0, p1, name="end_next",
    )
    a_wide1 = widen(a)
    qkv1, a_all1 = mix(a_wide1, near1, p1)
    away1 = move_core(qkv1)
    down1 = gather_slow(shards[2][1], qkv1)
    o1, lse1 = attend(qkv1, away1)
    up1 = sides(after(up1, o1))
    z1, x11, a2 = middle(narrow(proj(o1, near1)), y0, p1)
    a2_wide1 = widen(a2)
    down1 = sides(after(down1, x11))
    act1 = whole(up_kernel, act_out(), *a2_wide1, *up1, p1, name="up")

    w1, w0 = (near1, up1, down1), (near0, up0, down0)
    du, up_sums, dm_all, da2 = mlp_back(dm_wide1, act1, w1)
    g_down1 = pair_grad(dm_all, after(act1[0], da2[3]), after(act1[1], da2[3]))
    dx1, dz, mid = middle_back(hold(narrow(da2), g_down1), x11, cot, z1, p1)
    g_down1 = scatter_slow(g_down1)
    dz_wide = widen(dz)
    g_up1 = pair_grad(act1[4], after(du[0], dz), after(du[1], dz))
    m_parts = whole(
        pair_kernel, spread_out(), after(act1[0], da2[3]), act1[1], *down1, name="down"
    )
    dz_wide = hold(dz_wide, g_up1, m_parts[3])
    do, dz_all = back_to(dz_wide, near1)
    m_parts = narrow(lax.optimization_barrier((*m_parts, do))[:4])
    dq, nearby, far = attend_back(qkv1, away1, do, lse1)
    g_up1 = scatter_slow(g_up1)
    dqkv, sums, da = join_da(dq, nearby, after(move_core(far), g_down1, *m_parts), up_sums, near1)
    m1, y1 = whole(
        end_kernel, [out((TOK, D), F32), out((TOK, D), BF)], *m_parts, x11, p1, name="end"
    )
    g_near1 = near_grad(a_all1, dqkv, dz_all, after(o1, da[3]))
    send1, dx, dm0 = whole(
        next_back_kernel,
        [out((8, 176, 128), BF), out((TOK, D), BF), out((TOK, D), BF)],
        *hold(narrow(da), g_near1), y0, dx1, p1, cot, m1, mid, sums, y1, p0, name="next_back",
    )
    g_near1 = scatter_slow(g_near1)
    dm_wide0 = hold(widen(dm0), g_up1)
    du, up_sums, dm_all, da2 = mlp_back(dm_wide0, act0, w0)
    g_down0 = pair_grad(dm_all, after(act0[0], da2[3]), after(act0[1], da2[3]))
    dx1, dz, mid = middle_back(hold(narrow(da2), g_down0, g_near1), x10, dx, z0, p0)
    dz_wide = widen(dz)
    g_up0 = pair_grad(act0[4], after(du[0], dz), after(du[1], dz))
    dz_wide = hold(dz_wide, g_up0)
    do, dz_all = back_to(dz_wide, near0)
    g_pair0 = scatter(jnp.concatenate([g_up0, g_down0], 1), do)
    dq, nearby, far = attend_back(qkv0, away0, do, lse0)
    dqkv, sums, da = join_da(dq, nearby, move_core(far), up_sums, near0)
    da = narrow(da)
    g_near0 = add_up(scatter(near_grad(a_all0, dqkv, dz_all, after(o0, da[0])), da[1]))
    send0 = whole(
        last_back_kernel, out((8, 176, 128), BF),
        *da, x, dx1, p0, dx, m0, mid, sums, name="last_back",
    )

    g_near = to_owner(g_near0, g_near1.astype(F32))
    send0 = after(send0, g_near0)
    g_pair0 = add_up(after(g_pair0, send0))
    g_up = to_owner(g_pair0[:, :512], g_up1.astype(F32))
    g_down = to_owner(g_pair0[:, 512:], g_down1.astype(F32))

    got = lax.all_to_all(jnp.concatenate([send0, send1], 0), SS, 0, 0, tiled=True)
    ends_out = jnp.stack([got[s, :128] for s in SLOT]).reshape(9, 8, 16, 128)
    ends_out = jnp.transpose(ends_out, (2, 0, 1, 3)).reshape(16, 9, D)
    small = jnp.sum(got[:, 128:].astype(F32), 0)
    small = small[:24] + small[24:]
    both = move_core(small)
    vec = small[:8] + both[:8]
    vec = vec + move_x(vec, 1) + move_x(vec, -1) + move_x(vec, 2)
    g_vec = lax.dynamic_slice(vec, (0, ten * 16), (8, 16))
    bias = small[8:16] + both[16:24]
    qv = jnp.stack([bias[0].reshape(2, 64), bias[2].reshape(2, 64)], 1).reshape(4, 64)
    g_qvb = lax.dynamic_slice(qv, (0, seq * 8), (4, 8))
    g_upb = lax.dynamic_slice(bias[3:7].reshape(8, 64), (0, seq * 8), (8, 8))

    g_qkv = jnp.transpose(g_near[:, :384].reshape(128, 3, 2, HEAD), (0, 2, 1, 3)).reshape(128, 384)
    g_out = g_near[:, 384:].T
    return (
        ends_out[None],
        g_qkv[None],
        g_qvb[None],
        g_out[None],
        g_up[None],
        g_upb[None],
        g_down.T[None],
        g_vec[None],
    )


def solution(mesh):
    placed = (
        P("section", ("seq", "tensor"), None, None),
        P("section", "seq", "tensor"),
        P("section", "tensor", "seq"),
        P("section", "tensor", "seq"),
        P("section", "seq", "tensor"),
        P("section", "tensor", "seq"),
        P("section", "tensor", "seq"),
        P("section", None, ("seq", "tensor")),
    )
    return jax.shard_map(
        on_device, mesh=mesh, in_specs=placed, out_specs=placed, check_vma=False
    )
```

```python
import jax
import jax.numpy as jnp
from jax import lax
from jax.experimental import pallas as pl
from jax.experimental.pallas import tpu as pltpu
from jax.sharding import PartitionSpec as P

SS = ("section", "seq")
EPS = 1e-6
F32 = jnp.float32
BF = jnp.bfloat16
D = 1024
HEAD = 64
TOK = 128
GROUPS = [0, 1, 2, 3, 4, None, None, None, 5, 6, 7, 8, None, None, None, None]
SLOT = [GROUPS.index(i) for i in range(9)]


def move_x(v, d):
    return lax.ppermute(v, "tensor", [(i, (i + 2 * d) % 8) for i in range(8)])


def move_core(v):
    return lax.ppermute(v, "tensor", [(i, i ^ 1) for i in range(8)])


def move_section(v):
    return lax.ppermute(v, "section", [(0, 1), (1, 0)])


def widen(v):
    return v, move_x(v, 1), move_x(v, -1), move_x(v, 2)


def narrow(parts):
    own, back, ahead, far = parts
    return own, move_x(back, -1), move_x(ahead, 1), move_x(far, 2)


def dot(a, b, dims, out=F32):
    return lax.dot_general(a, b, (dims, ((), ())), preferred_element_type=F32).astype(out)


NN = ((1,), (0,))
NT = ((1,), (1,))
TN = ((0,), (0,))


def entire(a):
    zeros = (0,) * len(a.shape)
    return pl.BlockSpec(a.shape, lambda i: zeros, pipeline_mode=pl.Buffered(1))


def part(width, k):
    return pl.BlockSpec((1024, width), lambda i: (0, k), pipeline_mode=pl.Buffered(1))


def whole(kernel, out_shape, *args, name, cols=None):
    return pl.pallas_call(
        kernel,
        grid=(1,),
        out_shape=out_shape,
        in_specs=[entire(a) for a in args] if cols is None else [
            entire(a) if a.shape[1:] != (512,) or a.shape[0] != 1024 else part(*cols) for a in args
        ],
        out_specs=jax.tree.map(entire, out_shape),
        compiler_params=pltpu.CompilerParams(vmem_limit_bytes=60 * 2**20),
        cost_estimate=pl.CostEstimate(flops=0, bytes_accessed=4096, transcendentals=0),
        name=name,
    )(*args)


def out(shape, dtype):
    return jax.ShapeDtypeStruct(shape, dtype)


def row(p_ref, r):
    return jnp.concatenate([p_ref[q, r : r + 1, :] for q in range(8)], axis=1)


def bias_rows(p_ref, side):
    return sum(p_ref[q, 8 + 8 * side : 16 + 8 * side, :] for q in range(8))


def unit_of(v):
    centred = v - jnp.mean(v, axis=-1, keepdims=True)
    scale = lax.rsqrt(jnp.mean(centred * centred, axis=-1, keepdims=True) + EPS)
    return centred * scale, scale


def norm_back(v, gain, grad):
    unit, scale = unit_of(v)
    inner = grad * gain
    part = scale * (
        inner
        - jnp.mean(inner, axis=-1, keepdims=True)
        - unit * jnp.mean(inner * unit, axis=-1, keepdims=True)
    )
    return part, jnp.sum(grad * unit, 0, keepdims=True), jnp.sum(grad, 0, keepdims=True)


def total(own, back, ahead, far):
    return own[...] + back[...].astype(F32) + ahead[...].astype(F32) + far[...].astype(F32)


def start_kernel(x_ref, p_ref, a_ref):
    unit, _ = unit_of(x_ref[...].astype(F32))
    a_ref[...] = (unit * row(p_ref, 0) + row(p_ref, 1)).astype(BF)


def qkv_kernel(a0, a1, a2, a3, w0, w1, p_ref, o_ref, a_ref):
    join_rows((a0, a1, a2, a3), a_ref)
    mix_rows((a0, a1, a2, a3), w0, w1, p_ref, o_ref)


def mix_rows(pieces, w0, w1, p_ref, o_ref):
    for side, w in enumerate((w0, w1)):
        b = bias_rows(p_ref, side)
        b = jnp.concatenate([b[0:1], b[1:2], b[2:3]], axis=1)
        for i, a in enumerate(pieces):
            o_ref[128 * i : 128 * i + 128, 384 * side : 384 * side + 384] = (
                jnp.dot(a[...], w[...], preferred_element_type=F32) + b
            ).astype(BF)


def join_rows(pieces, ref):
    for i, piece in enumerate(pieces):
        ref[128 * i : 128 * i + 128, :] = piece[...]


def first_qkv_kernel(x0, x1, x2, x3, w0, w1, p_ref, o_ref, a_ref):
    pieces = [a_ref.at[128 * i : 128 * i + 128] for i in range(4)]
    for x, a in zip((x0, x1, x2, x3), pieces):
        start_kernel(x, p_ref, a)
    mix_rows(pieces, w0, w1, p_ref, o_ref)


def spread(left, own_ref, others):
    own_ref[...] = left(0)
    for i, ref in enumerate(others):
        ref[...] = left(i + 1).astype(BF)


def spread_out():
    return [out((TOK, D), F32)] + [out((TOK, D), BF)] * 3


def pair_kernel(l0, l1, w0, w1, own, back, ahead, far):
    def left(i):
        at = slice(128 * i, 128 * i + 128)
        return dot(l0[at, :], w0[...], NT) + dot(l1[at, :], w1[...], NT)

    spread(left, own, (back, ahead, far))


def proj_kernel(o, w0, w1, own, back, ahead, far):
    w = jnp.concatenate([w0[...], w1[...]], axis=1)
    spread(lambda i: dot(o[128 * i : 128 * i + 128, :], w, NT), own, (back, ahead, far))


def mixed_kernel(g, w0, w1, own, back, ahead, far):
    w = jnp.concatenate([w0[...], w1[...]], axis=1)
    spread(lambda i: dot(g[128 * i : 128 * i + 128, :], w, NT), own, (back, ahead, far))


def middle_kernel(own, back, ahead, far, x_ref, p_ref, z_ref, x1_ref, a2_ref):
    z = total(own, back, ahead, far) + row(p_ref, 4)
    x1 = x_ref[...].astype(F32) + row(p_ref, 6) * z
    unit, _ = unit_of(x1)
    z_ref[...] = z
    x1_ref[...] = x1
    a2_ref[...] = (unit * row(p_ref, 2) + row(p_ref, 3)).astype(BF)


def up_kernel(a0, a1, a2, a3, w0, w1, p_ref, act0, act1, slope0, slope1, a_ref):
    join_rows((a0, a1, a2, a3), a_ref)
    for side, (w, act, slope) in enumerate(((w0, act0, slope0), (w1, act1, slope1))):
        b = bias_rows(p_ref, side)
        b = jnp.concatenate([b[3:4], b[4:5], b[5:6], b[6:7]], axis=1)
        for i, a in enumerate((a0, a1, a2, a3)):
            at = slice(128 * i, 128 * i + 128)
            u = jnp.dot(a[...], w[...], preferred_element_type=F32) + b
            half = 0.5 * (1.0 + lax.erf(u * (0.5**0.5)))
            act[at, :] = (u * half).astype(BF)
            slope[at, :] = (half + u * jnp.exp(-0.5 * u * u) * 0.3989422804014327).astype(BF)


def mlp_kernel(
    a0, a1, a2, a3, u0, u1, d0, d1, p_ref, act0, act1, slope0, slope1, a_ref, own, back, ahead, far
):
    up_kernel(a0, a1, a2, a3, u0, u1, p_ref, act0, act1, slope0, slope1, a_ref)
    pair_kernel(act0, act1, d0, d1, own, back, ahead, far)


def mlp_back_kernel(
    d0, d1, d2, d3, w0, w1, u0, u1, s0, s1, du0, du1, sums, d_ref, own, back, ahead, far
):
    join_rows((d0, d1, d2, d3), d_ref)
    du_kernel(d0, d1, d2, d3, w0, w1, s0, s1, du0, du1, sums)
    pair_kernel(du0, du1, u0, u1, own, back, ahead, far)


def end_kernel(own, back, ahead, far, x1_ref, p_ref, m_ref, y_ref):
    m = total(own, back, ahead, far) + row(p_ref, 5)
    m_ref[...] = m
    y_ref[...] = (x1_ref[...] + row(p_ref, 7) * m).astype(BF)


def end_next_kernel(own, back, ahead, far, x1_ref, p_ref, next_ref, m_ref, y_ref, a_ref):
    end_kernel(own, back, ahead, far, x1_ref, p_ref, m_ref, y_ref)
    start_kernel(y_ref, next_ref, a_ref)


def turn_kernel(*refs):
    scale = row(refs[4], 7)
    for dy, dm in zip(refs[:4], refs[5:]):
        dm[...] = (scale * dy[...].astype(F32)).astype(BF)


def du_kernel(d0, d1, d2, d3, w0, w1, s0, s1, du0, du1, sums_ref):
    for side, (w, slope, du_ref) in enumerate(((w0, s0, du0), (w1, s1, du1))):
        acc = jnp.zeros((1, 512), F32)
        for i, d in enumerate((d0, d1, d2, d3)):
            at = slice(128 * i, 128 * i + 128)
            du = (jnp.dot(d[...], w[...], preferred_element_type=F32) * slope[at, :].astype(F32)).astype(BF)
            du_ref[at, :] = du
            acc = acc + jnp.sum(du.astype(F32), 0, keepdims=True)
        for k in range(4):
            sums_ref[side, k : k + 1, :] = acc[:, 128 * k : 128 * k + 128]
        sums_ref[side, 4:, :] = jnp.zeros((4, 128), F32)


def middle_back_kernel(own, back, ahead, far, x1_ref, dy_ref, z_ref, p_ref, dx1_ref, dz_ref, rows_ref):
    part, dg, db = norm_back(x1_ref[...], row(p_ref, 2), total(own, back, ahead, far))
    dx1 = dy_ref[...].astype(F32) + part
    scale = row(p_ref, 6)
    dx1_ref[...] = dx1
    dz_ref[...] = (scale * dx1).astype(BF)
    rows_ref[0:1, :] = dg
    rows_ref[1:2, :] = db
    rows_ref[2:3, :] = scale * jnp.sum(dx1, 0, keepdims=True)
    rows_ref[3:4, :] = jnp.sum(dx1 * z_ref[...], 0, keepdims=True)


def do_kernel(d0, d1, d2, d3, w0, w1, o_ref, d_ref):
    join_rows((d0, d1, d2, d3), d_ref)
    w = jnp.concatenate([w0[...], w1[...]], axis=1)
    for i, d in enumerate((d0, d1, d2, d3)):
        o_ref[128 * i : 128 * i + 128, :] = jnp.dot(d[...], w, preferred_element_type=F32).astype(BF)


def pack_out(out_ref, ends, vec, bias_ref):
    for q in range(8):
        for k in range(8):
            out_ref[q, 16 * k : 16 * k + 16, :] = ends[16 * q : 16 * q + 16, 128 * k : 128 * k + 128]
        part = [v[:, 128 * q : 128 * q + 128] for v in vec]
        part = jnp.concatenate(part + [bias_ref[0], bias_ref[1]], axis=0)
        high = part.astype(BF).astype(F32)
        out_ref[q, 128:176, :] = jnp.concatenate([high, part - high], axis=0).astype(BF)


def first_back(da, x_ref, dx1_ref, p_ref, dy_ref, m_ref, mid_ref):
    part, dg, db = norm_back(x_ref[...].astype(F32), row(p_ref, 0), total(*da))
    dy = dy_ref[...].astype(F32)
    vec = [
        dg, db, mid_ref[0:1, :], mid_ref[1:2, :], mid_ref[2:3, :],
        row(p_ref, 7) * jnp.sum(dy, 0, keepdims=True),
        mid_ref[3:4, :],
        jnp.sum(dy * m_ref[...], 0, keepdims=True),
    ]
    return (dx1_ref[...] + part).astype(BF), vec


def last_back_kernel(own, back, ahead, far, x, dx1, p, dy, m, mid, bias, out_ref):
    dx, vec = first_back((own, back, ahead, far), x, dx1, p, dy, m, mid)
    pack_out(out_ref, dx, vec, bias)


def next_back_kernel(
    own, back, ahead, far, x, dx1, p, dy, m, mid, bias, y_ref, next_ref, out_ref, dx_ref, dm_ref
):
    dx, vec = first_back((own, back, ahead, far), x, dx1, p, dy, m, mid)
    dx_ref[...] = dx
    dm_ref[...] = (row(next_ref, 7) * dx.astype(F32)).astype(BF)
    pack_out(out_ref, y_ref[...], vec, bias)


def attend_kernel(q_ref, k0_ref, v0_ref, k1_ref, v1_ref, o_ref, lse_ref):
    rows = q_ref.shape[0]
    lane = lax.broadcasted_iota(jnp.int32, (rows, 128), 1)
    k = jnp.concatenate([k0_ref[...], k1_ref[...]], 0)
    v = jnp.concatenate([v0_ref[...], v1_ref[...]], 0)
    q = q_ref[...] * jnp.asarray(0.125, BF)
    zero = jnp.zeros_like(q)
    outs = []
    for h in range(2):
        mine = (lane < HEAD) if h == 0 else (lane >= HEAD)
        qh = jnp.where(mine, q, zero)
        s = lax.dot_general(k, qh, (((1,), (1,)), ((), ())), preferred_element_type=F32)
        top = jnp.max(s, axis=0, keepdims=True)
        p = jnp.exp(s - top)
        total = jnp.sum(p, axis=0, keepdims=True)
        o = lax.dot_general(v, p.astype(BF), (((0,), (0,)), ((), ())), preferred_element_type=F32)
        outs.append(o * (1.0 / total))
        lse_ref[0, h : h + 1, :] = top + jnp.log(total)
    sub = lax.broadcasted_iota(jnp.int32, outs[0].shape, 0)
    o_ref[...] = jnp.where(sub < HEAD, outs[0], outs[1]).T.astype(BF)


def column(rows, part, swap=False, tall=False):
    if swap:
        return pl.BlockSpec((rows, 128), lambda p, r: (0, 3 * (1 - p) + part))
    if tall:
        return pl.BlockSpec((rows, 128), lambda p, r: (0, 3 * p + part))
    return pl.BlockSpec((rows, 128), lambda p, r: (r, 3 * p + part))


def attend(qkv, away):
    rows = 256
    n = qkv.shape[0]
    return pl.pallas_call(
        attend_kernel,
        grid=(2, n // rows),
        in_specs=[
            column(rows, 0),
            column(n, 1, tall=True), column(n, 2, tall=True),
            column(n, 1, swap=True), column(n, 2, swap=True),
        ],
        out_specs=[
            pl.BlockSpec((rows, 128), lambda p, r: (r, p)),
            pl.BlockSpec((1, 8, rows), lambda p, r: (p, 0, r)),
        ],
        out_shape=[
            jax.ShapeDtypeStruct((n, 256), BF),
            jax.ShapeDtypeStruct((2, 8, n), F32),
        ],
        compiler_params=pltpu.CompilerParams(vmem_limit_bytes=60 * 2**20),
        cost_estimate=pl.CostEstimate(flops=0, bytes_accessed=4096, transcendentals=0),
        name="attend",
    )(qkv, qkv, qkv, away, away)


def attend_back_kernel(
    q_ref, k0_ref, v0_ref, k1_ref, v1_ref, do_ref, lse_ref,
    dq_ref, near_ref, far_ref, dk_acc, dv_acc,
):
    r = pl.program_id(1)
    rows = q_ref.shape[0]
    n = k0_ref.shape[0]
    lane = lax.broadcasted_iota(jnp.int32, (rows, 128), 1)
    k = jnp.concatenate([k0_ref[...], k1_ref[...]], 0)
    v = jnp.concatenate([v0_ref[...], v1_ref[...]], 0)
    q = q_ref[...] * jnp.asarray(0.125, BF)
    do = do_ref[...]
    zero = jnp.zeros_like(q)
    dqs = []
    dk = jnp.zeros((2 * n, 128), F32)
    dv = jnp.zeros((2 * n, 128), F32)
    for h in range(2):
        mine = (lane < HEAD) if h == 0 else (lane >= HEAD)
        qh = jnp.where(mine, q, zero)
        doh = jnp.where(mine, do, zero)
        s = lax.dot_general(k, qh, (((1,), (1,)), ((), ())), preferred_element_type=F32)
        p = jnp.exp(s - lse_ref[0, h : h + 1, :])
        dv = dv + jnp.dot(p.astype(BF), doh, preferred_element_type=F32)
        dp = lax.dot_general(v, doh, (((1,), (1,)), ((), ())), preferred_element_type=F32)
        delta = jnp.sum(p * dp, axis=0, keepdims=True)
        ds = (p * (dp - delta)).astype(BF)
        dk = dk + jnp.dot(ds, qh, preferred_element_type=F32)
        dqs.append(
            lax.dot_general(k, ds, (((0,), (0,)), ((), ())), preferred_element_type=F32)
        )
    sub = lax.broadcasted_iota(jnp.int32, dqs[0].shape, 0)
    dq_ref[...] = (jnp.where(sub < HEAD, dqs[0], dqs[1]) * 0.125).T.astype(BF)

    @pl.when(r == 0)
    def _():
        dk_acc[...] = dk
        dv_acc[...] = dv

    @pl.when(r > 0)
    def _():
        dk_acc[...] += dk
        dv_acc[...] += dv

    @pl.when(r == pl.num_programs(1) - 1)
    def _():
        near_ref[:, :128] = dk_acc[:n]
        near_ref[:, 128:] = dv_acc[:n]
        far_ref[:, :128] = dk_acc[n:].astype(BF)
        far_ref[:, 128:] = dv_acc[n:].astype(BF)


def attend_back(qkv, away, do, lse):
    rows = 256
    n = qkv.shape[0]
    here = pl.BlockSpec((rows, 128), lambda p, r: (r, p))
    shape = jax.ShapeDtypeStruct
    return pl.pallas_call(
        attend_back_kernel,
        grid=(2, n // rows),
        in_specs=[
            column(rows, 0),
            column(n, 1, tall=True), column(n, 2, tall=True),
            column(n, 1, swap=True), column(n, 2, swap=True),
            here,
            pl.BlockSpec((1, 8, rows), lambda p, r: (p, 0, r)),
        ],
        out_specs=[
            here,
            pl.BlockSpec((n, 256), lambda p, r: (0, p)),
            pl.BlockSpec((n, 256), lambda p, r: (0, 1 - p)),
        ],
        out_shape=[shape((n, 256), BF), shape((n, 512), F32), shape((n, 512), BF)],
        scratch_shapes=[pltpu.VMEM((2 * n, 128), F32), pltpu.VMEM((2 * n, 128), F32)],
        compiler_params=pltpu.CompilerParams(vmem_limit_bytes=60 * 2**20),
        cost_estimate=pl.CostEstimate(flops=0, bytes_accessed=4096, transcendentals=0),
        name="attend_back",
    )(qkv, qkv, qkv, away, away, do, lse)


def join_da_kernel(dq, near, far_in, up, w0, w1, dqkv, sums, own, back, ahead, far):
    join_kernel(dq, near, far_in, up, dqkv, sums)
    mixed_kernel(dqkv, w0, w1, own, back, ahead, far)


def join_kernel(dq_ref, near_ref, far_ref, up_ref, out_ref, sums_ref):
    for p in range(2):
        dkv = (near_ref[:, 256 * p : 256 * p + 256] + far_ref[:, 256 * p : 256 * p + 256].astype(F32)).astype(BF)
        dq = dq_ref[:, 128 * p : 128 * p + 128]
        out_ref[:, 384 * p : 384 * p + 128] = dq
        out_ref[:, 384 * p + 128 : 384 * p + 384] = dkv
        sums_ref[p, 0:1, :] = jnp.sum(dq.astype(F32), 0, keepdims=True)
        kv = jnp.sum(dkv.astype(F32), 0, keepdims=True)
        sums_ref[p, 1:2, :] = kv[:, :128]
        sums_ref[p, 2:3, :] = kv[:, 128:]
        sums_ref[p, 3:7, :] = up_ref[p, 0:4, :]
        sums_ref[p, 7:8, :] = jnp.zeros((1, 128), F32)


MM = 2 * 512 * 1024 * 1024


def after(value, *events):
    return lax.optimization_barrier((value, *events))[0]


def gather(shard, *events):
    full = after(jnp.broadcast_to(shard[None], (8, 128, 512)), *events)
    return lax.all_to_all(full, "seq", 0, 0, tiled=True).reshape(1024, 512)


def gather_slow(shard, *events):
    return lax.all_gather(after(shard, *events), "seq", axis=0, tiled=True)


def scatter_slow(g):
    return lax.psum_scatter(g, "seq", scatter_dimension=0, tiled=True)


def sides(full):
    return full, move_core(full)


def scatter(g, *events):
    return lax.all_to_all(after(g, *events), "seq", 0, 0, tiled=True).reshape(8, 128, 512)


def add_up(blocks):
    return jnp.sum(blocks.astype(F32), 0)


def core_sum(own, other):
    return (own + move_core(other).astype(F32)).astype(BF)


def hold(parts, *events):
    return (*parts[:-1], after(parts[-1], *events))


def mix(a_wide, near, p):
    return whole(qkv_kernel, [out((512, 768), BF), all_rows()], *a_wide, *near, p, name="qkv", cols=(384, 0))


def mix_first(x_wide, near, p):
    shapes = [out((512, 768), BF), all_rows()]
    return whole(first_qkv_kernel, shapes, *x_wide, *near, p, name="first_qkv", cols=(384, 0))


def proj(o, near):
    return whole(proj_kernel, spread_out(), o, *near, name="proj", cols=(128, 3))


def middle(z, x, p):
    return whole(
        middle_kernel, [out((TOK, D), F32)] * 2 + [out((TOK, D), BF)], *z, x, p, name="middle"
    )


def all_rows():
    return out((512, D), BF)


def act_out():
    return [out((512, 512), BF)] * 4 + [all_rows()]


def mlp_back(dm_wide, act, w):
    _, up, down = w
    *du, sums, dm_all, own, back, ahead, far = whole(
        mlp_back_kernel,
        [out((512, 512), BF)] * 2 + [out((2, 8, 128), F32), all_rows()] + spread_out(),
        *dm_wide, *down, *up, *act[2:4], name="mlp_back",
    )
    return du, sums, dm_all, (own, back, ahead, far)


def middle_back(da2, x1, dy, z, p):
    return whole(
        middle_back_kernel, [out((TOK, D), F32), out((TOK, D), BF), out((4, D), F32)],
        *da2, x1, dy, z, p, name="middle_back",
    )


def pair_grad(rows, left, right):
    return core_sum(dot(rows, left, TN), dot(rows, right, TN, BF))


def near_grad(a_all, dqkv, dz_all, o):
    own = jnp.concatenate([dot(a_all, dqkv[:, :384], TN), dot(dz_all, o[:, :128], TN)], 1)
    other = jnp.concatenate(
        [dot(a_all, dqkv[:, 384:], TN, BF), dot(dz_all, o[:, 128:], TN, BF)], 1
    )
    return core_sum(own, other)


def back_to(dz_wide, near):
    return whole(do_kernel, [out((512, 256), BF), all_rows()], *dz_wide, *near, name="do", cols=(128, 3))


def join_da(dq, nearby, far, up_sums, near):
    dqkv, sums, *da = whole(
        join_da_kernel,
        [out((512, 768), BF), out((2, 8, 128), F32)] + spread_out(),
        dq, nearby, far, up_sums, *near, name="join_da", cols=(384, 0),
    )
    return dqkv, sums, da


def on_device(ends, w_qkv, qv_bias, w_proj, w_fc1, fc1_bias, w_fc2, vectors):
    sec = lax.axis_index("section")
    seq = lax.axis_index("seq")
    ten = lax.axis_index("tensor")
    first = sec == 0

    lane = jnp.arange(128)[None, :]
    vec = jnp.where(lane // 16 == ten, jnp.tile(vectors[0], (1, 8)), 0.0)
    here = (jnp.arange(8) == seq).astype(F32)[None, :, None]
    qv = qv_bias[0].astype(F32).reshape(2, 2, 8)
    qv = jnp.stack([qv[:, 0], jnp.zeros((2, 8), F32), qv[:, 1]])
    qv = (qv.reshape(6, 1, 8) * here).reshape(3, 128)
    fb = (fc1_bias[0].astype(F32)[:, None, :] * here).reshape(4, 128)
    bias = jnp.concatenate([qv, fb, jnp.zeros((1, 128), F32)], 0)
    both = move_core(jnp.concatenate([vec, bias], 0))
    small = jnp.concatenate([vec + both[:8], bias, both[8:]], 0)
    high = lax.reduce_precision(small, 8, 7)
    mid = lax.reduce_precision(small - high, 8, 7)
    parts = jnp.concatenate([high, mid, small - high - mid, jnp.zeros((8, 128), F32)], 0).astype(BF)

    by_image = jnp.transpose(ends[0].reshape(16, 9, 8, 128), (1, 2, 0, 3)).reshape(9, 128, 128)
    blank = jnp.zeros((128, 128), BF)
    send = jnp.stack([blank if g is None else by_image[g] for g in GROUPS])
    send = jnp.concatenate([send, jnp.broadcast_to(parts[None], (16, 80, 128))], 1)
    got = lax.all_to_all(send, SS, 0, 0, tiled=True)
    x, cot = (
        jnp.transpose(v.reshape(8, 8, 16, 128), (0, 2, 1, 3)).reshape(TOK, D)
        for v in (got[:8, :128], got[8:, :128])
    )
    small = got[:, 128:].astype(F32)
    small = small[:, :24] + small[:, 24:48] + small[:, 48:72]
    vec = small[:, :8]
    vec = vec + move_x(vec, 1) + move_x(vec, -1) + move_x(vec, 2)
    pars = jnp.concatenate([vec, small[:, 8:]], 1)
    p0, p1 = pars[:8], pars[8:]

    own_qkv = jnp.transpose(w_qkv[0].reshape(128, 2, 3, HEAD), (0, 2, 1, 3)).reshape(128, 384)
    shard = jnp.concatenate([own_qkv, w_proj[0].T, w_fc1[0], w_fc2[0].T], 1)
    moved = move_section(shard)
    shards = jnp.where(first, shard, moved), jnp.where(first, moved, shard)
    shards = [[v[:, 512 * k : 512 * k + 512] for v in shards] for k in range(3)]

    def to_owner(a, b):
        other = move_section(jnp.where(first, b, a).astype(BF)).astype(F32)
        return jnp.where(first, a, b) + other

    near0 = gather(shards[0][0], got)
    x_wide0 = widen(x)
    cot_wide = widen(after(cot, *x_wide0))
    near0 = sides(after(near0, p0, *x_wide0))
    qkv0, a_all0 = mix_first(x_wide0, near0, p0)
    away0 = move_core(qkv0)
    up0 = gather(shards[1][0], near0[0], p0)
    o0, lse0 = attend(qkv0, away0)
    dm_wide1 = whole(turn_kernel, [out((TOK, D), BF)] * 4, *cot_wide, p1, name="turn")
    z = proj(after(o0, *cot_wide), near0)
    down0 = gather(shards[2][0], up0, z[3])
    near1 = gather_slow(shards[0][1], z[3])
    up0 = sides(after(up0, z[3]))
    z0, x10, a2 = middle(narrow(z), x, p0)
    down0 = sides(after(down0, x10))
    a2_wide0 = widen(a2)
    *act0, o_, b_, a_, f_ = whole(
        mlp_kernel, act_out() + spread_out(), *a2_wide0, *up0, *down0, p0,
        name="mlp",
    )
    near1 = sides(after(near1, f_))
    up1 = gather_slow(shards[1][1], f_)
    m0, y0, a = whole(
        end_next_kernel, [out((TOK, D), F32), out((TOK, D), BF), out((TOK, D), BF)],
        *narrow((o_, b_, a_, f_)), x10, p0, p1, name="end_next",
    )
    a_wide1 = widen(a)
    qkv1, a_all1 = mix(a_wide1, near1, p1)
    away1 = move_core(qkv1)
    down1 = gather_slow(shards[2][1], qkv1)
    o1, lse1 = attend(qkv1, away1)
    up1 = sides(after(up1, o1))
    z1, x11, a2 = middle(narrow(proj(o1, near1)), y0, p1)
    a2_wide1 = widen(a2)
    down1 = sides(after(down1, x11))
    act1 = whole(up_kernel, act_out(), *a2_wide1, *up1, p1, name="up")

    w1, w0 = (near1, up1, down1), (near0, up0, down0)
    du, up_sums, dm_all, da2 = mlp_back(dm_wide1, act1, w1)
    g_down1 = pair_grad(dm_all, after(act1[0], da2[3]), after(act1[1], da2[3]))
    dx1, dz, mid = middle_back(hold(narrow(da2), g_down1), x11, cot, z1, p1)
    g_down1 = scatter_slow(g_down1)
    dz_wide = widen(dz)
    g_up1 = pair_grad(act1[4], after(du[0], dz), after(du[1], dz))
    m_parts = whole(
        pair_kernel, spread_out(), after(act1[0], da2[3]), act1[1], *down1, name="down"
    )
    dz_wide = hold(dz_wide, g_up1, m_parts[3])
    do, dz_all = back_to(dz_wide, near1)
    m_parts = narrow(lax.optimization_barrier((*m_parts, do))[:4])
    dq, nearby, far = attend_back(qkv1, away1, do, lse1)
    g_up1 = scatter_slow(g_up1)
    dqkv, sums, da = join_da(dq, nearby, after(move_core(after(far, *m_parts)), g_down1), up_sums, near1)
    m1, y1 = whole(
        end_kernel, [out((TOK, D), F32), out((TOK, D), BF)], *m_parts, x11, p1, name="end"
    )
    g_near1 = near_grad(a_all1, dqkv, dz_all, after(o1, da[3]))
    send1, dx, dm0 = whole(
        next_back_kernel,
        [out((8, 176, 128), BF), out((TOK, D), BF), out((TOK, D), BF)],
        *hold(narrow(da), g_near1), y0, dx1, p1, cot, m1, mid, sums, y1, p0, name="next_back",
    )
    g_near1 = scatter_slow(g_near1)
    dm_wide0 = hold(widen(dm0), g_up1)
    du, up_sums, dm_all, da2 = mlp_back(dm_wide0, act0, w0)
    g_down0 = pair_grad(dm_all, after(act0[0], da2[3]), after(act0[1], da2[3]))
    dx1, dz, mid = middle_back(hold(narrow(da2), g_down0, g_near1), x10, dx, z0, p0)
    g_down0 = scatter_slow(g_down0)
    dz_wide = widen(dz)
    g_up0 = pair_grad(act0[4], after(du[0], dz), after(du[1], dz))
    dz_wide = hold(dz_wide, g_up0)
    do, dz_all = back_to(dz_wide, near0)
    g_up0 = scatter(g_up0, do)
    dq, nearby, far = attend_back(qkv0, away0, do, lse0)
    dqkv, sums, da = join_da(dq, nearby, after(move_core(far), g_up0), up_sums, near0)
    da = narrow(da)
    g_near0 = add_up(scatter(near_grad(a_all0, dqkv, dz_all, after(o0, da[0])), g_down0, *da[1:]))
    send0 = whole(
        last_back_kernel, out((8, 176, 128), BF),
        *da, x, dx1, p0, dx, m0, mid, sums, name="last_back",
    )

    g_near = to_owner(g_near0, g_near1.astype(F32))
    send0 = after(send0, g_near0)
    g_up = to_owner(add_up(after(g_up0, send0)), g_up1.astype(F32))
    g_down = to_owner(after(g_down0, send0).astype(F32), g_down1.astype(F32))

    got = lax.all_to_all(jnp.concatenate([send0, send1], 0), SS, 0, 0, tiled=True)
    ends_out = jnp.stack([got[s, :128] for s in SLOT]).reshape(9, 8, 16, 128)
    ends_out = jnp.transpose(ends_out, (2, 0, 1, 3)).reshape(16, 9, D)
    small = jnp.sum(got[:, 128:].astype(F32), 0)
    small = small[:24] + small[24:]
    both = move_core(small)
    vec = small[:8] + both[:8]
    vec = vec + move_x(vec, 1) + move_x(vec, -1) + move_x(vec, 2)
    g_vec = lax.dynamic_slice(vec, (0, ten * 16), (8, 16))
    bias = small[8:16] + both[16:24]
    qv = jnp.stack([bias[0].reshape(2, 64), bias[2].reshape(2, 64)], 1).reshape(4, 64)
    g_qvb = lax.dynamic_slice(qv, (0, seq * 8), (4, 8))
    g_upb = lax.dynamic_slice(bias[3:7].reshape(8, 64), (0, seq * 8), (8, 8))

    g_qkv = jnp.transpose(g_near[:, :384].reshape(128, 3, 2, HEAD), (0, 2, 1, 3)).reshape(128, 384)
    g_out = g_near[:, 384:].T
    return (
        ends_out[None],
        g_qkv[None],
        g_qvb[None],
        g_out[None],
        g_up[None],
        g_upb[None],
        g_down.T[None],
        g_vec[None],
    )


def solution(mesh):
    placed = (
        P("section", ("seq", "tensor"), None, None),
        P("section", "seq", "tensor"),
        P("section", "tensor", "seq"),
        P("section", "tensor", "seq"),
        P("section", "seq", "tensor"),
        P("section", "tensor", "seq"),
        P("section", "tensor", "seq"),
        P("section", None, ("seq", "tensor")),
    )
    return jax.shard_map(
        on_device, mesh=mesh, in_specs=placed, out_specs=placed, check_vma=False
    )
```
